256 devices in a mesh: ia: 8 (over x, y_lo), ja: 4 (over y_hi, core), ka: 8 (over z).
Axes of the slice: x: 4, y: 4 (y_hi: 2, y_lo: 2; y = y_hi * 2 + y_lo), z: 8, core: 2. Of those that a mesh axis runs over, the one named last changes fastest.
Arguments:
- pre_act: bfloat16 [4096, 24576], P('ia', ('ja', 'ka')), may hold values from -6 to 6
- down_weight: bfloat16 [6144, 24576], P(('ka', 'ia'), 'ja'), may hold values from -0.109375 to 0.109375
- grad_out: bfloat16 [4096, 6144], P('ia', ('ka', 'ja')), may hold values from -6 to 6
Outputs:
- output: bfloat16 [4096, 6144], P('ia', ('ka', 'ja'))
- grad_pre: bfloat16 [4096, 24576], P('ia', ('ja', 'ka'))
- grad_weight: bfloat16 [6144, 24576], P(('ka', 'ia'), 'ja')
The draws below stay inside these ranges and needn't reach their ends.
All inputs are finite; a program needn't handle non-finite values.
Results may differ from the reference program's by a relative error of at most 0.02.
Values may be sent and summed in bfloat16 or wider, within the bound.
No kernel may reach another device: no remote copies, remote signals or barrier semaphores. Data moves between devices by JAX's collectives and lax.ppermute only.
A program may use at most 128 MiB of HBM per device.

```python
import jax
import jax.numpy as jnp
from jax import lax

D = 6144
FF = 24576
TOK_DEV = 512
TOKENS = 4096
N_IA = 8
N_KA = 8


def strengthened(result, stream_key, source, target, parts, factor):
    def block_of(dim):
        return (jnp.arange(result.shape[dim]) // (result.shape[dim] // parts)).reshape((-1,) + (1,) * (result.ndim - 1 - dim))

    one_side = jax.random.permutation(stream_key, parts)[block_of(target)]
    far = (block_of(target) + parts // 2) % parts
    return jnp.where((block_of(source) == one_side) | (block_of(source) == far), factor * result, result)


def levels(key, extent, split, least, high):
    def one(dim, parts):
        steps = jax.random.uniform(jax.random.fold_in(jax.random.fold_in(key, 6), dim), (parts,), jnp.float32, least / len(split), high / len(split))
        return jnp.repeat(jnp.exp(steps), extent[dim] // parts).reshape((-1,) + (1,) * (len(extent) - dim - 1))

    gain = one(*split[0])
    for cut in split[1:]:
        gain = gain * one(*cut)
    return gain


def bell_draw(stream_key, shape, scale, bound, split=(), held_as=jnp.bfloat16):
    result = scale * jax.random.normal(stream_key, shape, jnp.float32)
    if split:
        result = result * levels(stream_key, shape, split, -0.22, 0.18)
    return jnp.clip(result, -bound, bound).astype(held_as)


def noise_with(stream_key, shape, deviation, bound, cuts, heavy, dtype=jnp.bfloat16):
    result = deviation * jax.random.normal(stream_key, shape, jnp.float32)
    if cuts:
        result = result * levels(stream_key, shape, cuts, -0.22, 0.18)
    return jnp.clip(strengthened(result, jax.random.fold_in(stream_key, 3), *heavy), -bound, bound).astype(dtype)


def setup_inputs(seed: int = 0) -> dict:
    streams_of = jax.random.split(jax.random.key(seed), 4)
    return {
        "pre_act": bell_draw(streams_of[0], (TOKENS, FF), 1.0, 6.0, ((0, 8), (1, 32))),
        "down_weight": noise_with(streams_of[1], (D, FF), FF ** -0.5, 0.109375, ((0, 64), (1, 4)), (0, 1, 64, 4.0)),
        "grad_out": noise_with(streams_of[2], (TOKENS, D), 1.0, 6.0, ((0, 8), (1, 32)), (0, 1, 32, 2.75)),
    }


coeff = 0.7978845608028654


def gelu_value(v):
    return 0.5 * v * (1.0 + jnp.tanh(coeff * (v + 0.044715 * v * v * v)))


def gelu_slope(v):
    tval = jnp.tanh(coeff * (v + 0.044715 * v * v * v))
    return 0.5 * (1.0 + tval) + 0.5 * v * (1.0 - tval * tval) * coeff * (1.0 + 3.0 * 0.044715 * v * v)


def reference(pre_act, down_weight, grad_out):
    pre32 = pre_act.astype(jnp.float32)
    hidden = gelu_value(pre32).astype(jnp.bfloat16)
    output = lax.dot_general(hidden, down_weight, (((1,), (1,)), ((), ())), preferred_element_type=jnp.float32).astype(jnp.bfloat16)
    width = D // N_KA
    grad_hidden = jnp.zeros((TOKENS, FF), jnp.float32)
    for block in range(N_KA):
        cols = grad_out[:, block * width:(block + 1) * width]
        wrows = down_weight[block * width:(block + 1) * width]
        part = jnp.dot(cols, wrows, preferred_element_type=jnp.float32)
        grad_hidden = grad_hidden + part.astype(jnp.bfloat16).astype(jnp.float32)
    grad_pre = (grad_hidden * gelu_slope(pre32)).astype(jnp.bfloat16)
    grad_weight = jnp.zeros((D, FF), jnp.float32)
    for block in range(N_IA):
        rows = hidden[block * TOK_DEV:(block + 1) * TOK_DEV]
        grows = grad_out[block * TOK_DEV:(block + 1) * TOK_DEV]
        part = lax.dot_general(grows, rows, (((0,), (0,)), ((), ())), preferred_element_type=jnp.float32)
        grad_weight = grad_weight + part.astype(jnp.bfloat16).astype(jnp.float32)
    return output, grad_pre, grad_weight.astype(jnp.bfloat16)
```

```python
import jax
import jax.numpy as jnp
from jax import lax
from jax.experimental import pallas as pl
from jax.experimental.pallas import tpu as pltpu
from jax.sharding import Mesh
from jax.sharding import PartitionSpec as P

coeff = 0.7978845608028654
bf16 = jnp.bfloat16
f32 = jnp.float32


def gelu_value(v):
    return 0.5 * v * (1.0 + jnp.tanh(coeff * (v + 0.044715 * v * v * v)))


def gelu_slope(v):
    tval = jnp.tanh(coeff * (v + 0.044715 * v * v * v))
    return 0.5 * (1.0 + tval) + 0.5 * v * (1.0 - tval * tval) * coeff * (
        1.0 + 3.0 * 0.044715 * v * v
    )


def swap_y(a, mask):
    flip = (mask & 1) * 2 + (mask >> 1)
    return lax.ppermute(a, ("yl", "yh"), [(i, i ^ flip) for i in range(4)])


def swap_x(a, mask):
    return lax.ppermute(a, "x", [(i, i ^ mask) for i in range(4)])


def swap_c(a):
    return lax.ppermute(a, "c", [(0, 1), (1, 0)])


def near4(swap, own):
    return swap(own, 1), swap(own, 3)


def far4(swap, near1, near3):
    half = near1.shape[0] // 2
    return swap(near1[:half], 3), swap(near3[half:], 1)


def add(a, b):
    return (a.astype(f32) + b.astype(f32)).astype(bf16)


def scatter_far(swap, far):
    half = far.shape[0] // 2
    return swap(far[:half], 1), swap(far[half:], 3)


def scatter_near(swap, near1, near3, far1, far3):
    half = far1.shape[0]
    near3 = jnp.concatenate([add(near3[:half], far1), near3[half:]], axis=0)
    near1 = jnp.concatenate([near1[:half], add(near1[half:], far3)], axis=0)
    return swap(near1, 1), swap(near3, 3)


def add3(own, got1, got3):
    return own.astype(f32) + got1.astype(f32) + got3.astype(f32)


def after(value, *others):
    return lax.optimization_barrier((value,) + others)[0]


def split_kernel(which_ref, a_ref, mine_ref, theirs_ref):
    which = which_ref[0]
    for value, low_ref, high_ref in ((0, mine_ref, theirs_ref), (1, theirs_ref, mine_ref)):

        @pl.when(which == value)
        def _(low_ref=low_ref, high_ref=high_ref):
            for k in range(a_ref.shape[1] // 768):
                low_ref[:, 384 * k : 384 * k + 384] = a_ref[:, 768 * k : 768 * k + 384]
                high_ref[:, 384 * k : 384 * k + 384] = a_ref[:, 768 * k + 384 : 768 * k + 768]


def split_columns(a, which):
    half = jax.ShapeDtypeStruct((a.shape[0], a.shape[1] // 2), a.dtype)
    return pl.pallas_call(
        split_kernel,
        out_shape=(half, half),
        in_specs=[pl.BlockSpec(memory_space=pltpu.SMEM), pl.BlockSpec(memory_space=pltpu.VMEM)],
        out_specs=(pl.BlockSpec(memory_space=pltpu.VMEM),) * 2,
        cost_estimate=pl.CostEstimate(flops=0, bytes_accessed=4 * a.size, transcendentals=0),
    )(which.astype(jnp.int32).reshape(1), a)


def join_columns(mine, theirs, which):
    low = jnp.where(which == 0, mine, theirs)
    high = jnp.where(which == 0, theirs, mine)
    n = mine.shape[1] // 384
    return jnp.concatenate([p[:, 384 * k : 384 * k + 384] for k in range(n) for p in (low, high)], axis=1)


def shards(pre_act, down_weight, grad_out):
    x, yl, yh, c = (lax.axis_index(n) for n in ("x", "yl", "yh", "c"))
    pre32 = pre_act.astype(f32)
    hid = gelu_value(pre32).astype(bf16)
    low, high = hid[:, :384], hid[:, 384:]
    keep, give = jnp.where(yl == 0, low, high), jnp.where(yl == 0, high, low)
    hidden = [lax.all_gather(keep, "z", axis=1, tiled=True)]
    got_h = swap_y(give, 1)
    hidden.append(lax.all_gather(got_h, "z", axis=1, tiled=True))

    keep, give = split_columns(down_weight, yl)
    own = jnp.concatenate([keep, swap_y(give, 1)], axis=0)
    near = near4(swap_x, own)
    weight = jnp.concatenate([own, near[0], *far4(swap_x, *near), near[1]], axis=0)

    small = grad_out.T
    got = [small] + [swap_y(small, m) for m in (1, 2, 3)]
    part = jnp.stack([jnp.concatenate([got[2 * h], got[2 * h + 1]], axis=1) for h in range(2)])
    table = jnp.concatenate([part, swap_c(part)], axis=0).reshape(8, 96, 1024)
    flip = x ^ (yh * 2 + c)
    iota = jnp.arange(8, dtype=jnp.int32)
    place = flip ^ (iota >> 1)
    grads = table[(place & 1) * 4 + (place >> 1) * 2 + (yl ^ (iota & 1))].reshape(768, 1024)
    grads = [grads[:, :512], grads[:, 512:]]

    gh = []
    for t in (1, 0):
        part = lax.dot_general(weight, grads[t], (((0,), (0,)), ((), ())), preferred_element_type=f32).astype(bf16)
        part = after(part, hidden[1], *gh)
        gh.append(lax.psum_scatter(part, "z", scatter_dimension=0, tiled=True))
    mine, theirs = gh[1].T, swap_y(gh[0], 1).T
    grad_hidden = join_columns(mine, theirs, yl)
    grad_pre = (grad_hidden.astype(f32) * gelu_slope(pre32)).astype(bf16)

    gw = sum(jnp.dot(grads[t], hidden[t], preferred_element_type=f32) for t in range(2))
    gw = gw.astype(bf16).reshape(4, 192, 3072)
    sent = scatter_far(swap_x, gw[2])
    total = add3(gw[0], *scatter_near(swap_x, gw[1], gw[3], *sent)).astype(bf16)
    grad_weight = join_columns(total[:96], swap_y(total[96:], 1), yl)

    order = (flip ^ (((iota >> 1) & 1) * 2 + (iota >> 2))) * 2 + ((iota & 1) ^ yl)
    total = jnp.zeros((192, 512), f32)
    for t in (1, 0):
        out = lax.dot_general(weight, after(hidden[t], gw), (((1,), (1,)), ((), ())), preferred_element_type=f32)
        out = out.astype(bf16).reshape(8, 96, 512)
        part = add(out[order[:4]], swap_c(out[order[4:]])).reshape(2, 192, 512)
        for h in (1, 0):
            total = total + (swap_y(part[h], 2 * h + t) if h + t else part[h]).astype(f32)
    output = total.astype(bf16).T
    return output, grad_pre, grad_weight


def solution(mesh):
    cube = Mesh(mesh.devices.reshape(4, 2, 2, 2, 8), ("x", "yl", "yh", "c", "z"))
    t, f, d = ("x", "yl"), ("yh", "c", "z"), ("z", "x", "yl")
    e = ("z", "yh", "c")
    return jax.shard_map(
        shards,
        mesh=cube,
        in_specs=(P(t, f), P(d, ("yh", "c")), P(t, e)),
        out_specs=(P(t, e), P(t, f), P(d, ("yh", "c"))),
        check_vma=False,
    )
```

```python
import jax
import jax.numpy as jnp
from jax import lax
from jax.experimental import pallas as pl
from jax.experimental.pallas import tpu as pltpu
from jax.sharding import Mesh
from jax.sharding import PartitionSpec as P

coeff = 0.7978845608028654
bf16 = jnp.bfloat16
f32 = jnp.float32


def gelu_value(v):
    return 0.5 * v * (1.0 + jnp.tanh(coeff * (v + 0.044715 * v * v * v)))


def gelu_slope(v):
    tval = jnp.tanh(coeff * (v + 0.044715 * v * v * v))
    return 0.5 * (1.0 + tval) + 0.5 * v * (1.0 - tval * tval) * coeff * (
        1.0 + 3.0 * 0.044715 * v * v
    )


def swap_y(a, mask):
    flip = (mask & 1) * 2 + (mask >> 1)
    return lax.ppermute(a, ("yl", "yh"), [(i, i ^ flip) for i in range(4)])


def swap_x(a, mask):
    return lax.ppermute(a, "x", [(i, i ^ mask) for i in range(4)])


def swap_c(a):
    return lax.ppermute(a, "c", [(0, 1), (1, 0)])


def gather4(swap, own):
    return [own] + [swap(own, m) for m in (1, 2, 3)]


def scatter4(swap, blocks):
    total = blocks[0].astype(f32)
    for m in (1, 3, 2):
        total = total + swap(blocks[m], m).astype(f32)
    return total.astype(bf16)


def add(a, b):
    return (a.astype(f32) + b.astype(f32)).astype(bf16)


def near4(swap, own):
    return swap(own, 1), swap(own, 3)


def far4(swap, near1, near3):
    half = near1.shape[0] // 2
    return swap(near1[:half], 3), swap(near3[half:], 1)


def scatter_far(swap, far):
    half = far.shape[0] // 2
    return swap(far[:half], 1), swap(far[half:], 3)


def scatter_near(swap, near1, near3, far1, far3):
    half = far1.shape[0]
    near3 = jnp.concatenate([add(near3[:half], far1), near3[half:]], axis=0)
    near1 = jnp.concatenate([near1[:half], add(near1[half:], far3)], axis=0)
    return swap(near1, 1), swap(near3, 3)


def add3(own, got1, got3):
    return own.astype(f32) + got1.astype(f32) + got3.astype(f32)


def after(value, *others):
    return lax.optimization_barrier((value,) + others)[0]


def split_kernel(which_ref, a_ref, mine_ref, theirs_ref):
    which = which_ref[0]
    for value, low_ref, high_ref in ((0, mine_ref, theirs_ref), (1, theirs_ref, mine_ref)):

        @pl.when(which == value)
        def _(low_ref=low_ref, high_ref=high_ref):
            for k in range(a_ref.shape[1] // 768):
                low_ref[:, 384 * k : 384 * k + 384] = a_ref[:, 768 * k : 768 * k + 384]
                high_ref[:, 384 * k : 384 * k + 384] = a_ref[:, 768 * k + 384 : 768 * k + 768]


def split_columns(a, which):
    half = jax.ShapeDtypeStruct((a.shape[0], a.shape[1] // 2), a.dtype)
    return pl.pallas_call(
        split_kernel,
        out_shape=(half, half),
        in_specs=[pl.BlockSpec(memory_space=pltpu.SMEM), pl.BlockSpec(memory_space=pltpu.VMEM)],
        out_specs=(pl.BlockSpec(memory_space=pltpu.VMEM),) * 2,
        cost_estimate=pl.CostEstimate(flops=0, bytes_accessed=4 * a.size, transcendentals=0),
    )(which.astype(jnp.int32).reshape(1), a)


def join_columns(mine, theirs, which):
    low = jnp.where(which == 0, mine, theirs)
    high = jnp.where(which == 0, theirs, mine)
    n = mine.shape[1] // 384
    return jnp.concatenate([p[:, 384 * k : 384 * k + 384] for k in range(n) for p in (low, high)], axis=1)


def shards(pre_act, down_weight, grad_out):
    x, yl, yh, c = (lax.axis_index(n) for n in ("x", "yl", "yh", "c"))
    pre32 = pre_act.astype(f32)
    hid = gelu_value(pre32).astype(bf16)
    low, high = hid[:, :384], hid[:, 384:]
    keep, give = jnp.where(yl == 0, low, high), jnp.where(yl == 0, high, low)
    got_h = swap_y(give, 1)

    keep_w, give_w = split_columns(after(down_weight, give), yl)
    got_w = swap_y(give_w, 1)
    hidden = lax.all_gather(jnp.concatenate([keep, after(got_h, keep_w)], axis=0), "z", axis=1, tiled=True)
    own = jnp.concatenate([keep_w, got_w], axis=0)
    near = near4(swap_x, after(own, got_h))
    weight = jnp.concatenate([own, near[0], *far4(swap_x, *near), near[1]], axis=0)

    got = gather4(swap_y, after(grad_out.T, near[0]))
    part = jnp.stack([jnp.concatenate([got[2 * h], got[2 * h + 1]], axis=1) for h in range(2)])
    table = jnp.concatenate([part, swap_c(part)], axis=0).reshape(8, 96, 1024)
    flip = x ^ (yh * 2 + c)
    iota = jnp.arange(8, dtype=jnp.int32)
    place = flip ^ (iota >> 1)
    grads = table[(place & 1) * 4 + (place >> 1) * 2 + (yl ^ (iota & 1))].reshape(768, 1024)

    gh = lax.dot_general(weight, grads, (((0,), (0,)), ((), ())), preferred_element_type=f32).astype(bf16)
    gh_z = lax.psum_scatter(after(gh, hidden), "z", scatter_dimension=0, tiled=True)
    grad_hidden = join_columns(gh_z[:, :512].T, swap_y(gh_z[:, 512:], 1).T, yl)
    grad_pre = (grad_hidden.astype(f32) * gelu_slope(pre32)).astype(bf16)

    gw_all = jnp.dot(after(grads, gh), hidden, preferred_element_type=f32).astype(bf16)
    gw = gw_all.reshape(4, 192, 3072)
    far = scatter_far(swap_x, gw[2])
    near = scatter_near(swap_x, gw[1], gw[3], *far)
    order = (flip ^ (((iota >> 1) & 1) * 2 + (iota >> 2))) * 2 + ((iota & 1) ^ yl)
    out = lax.dot_general(weight, after(hidden, gw_all, *far), (((1,), (1,)), ((), ())), preferred_element_type=f32)
    out = out.astype(bf16).reshape(8, 96, 1024)
    part = add(out[order[:4]], swap_c(out[order[4:]])).reshape(2, 192, 1024)
    output = scatter4(swap_y, [part[m >> 1, :, (m & 1) * 512 : (m & 1) * 512 + 512] for m in range(4)])

    total = add3(after(gw[0], output), *near).astype(bf16)
    grad_weight = join_columns(total[:96], swap_y(total[96:], 1), yl)
    output = output.T
    return output, grad_pre, grad_weight


def solution(mesh):
    cube = Mesh(mesh.devices.reshape(4, 2, 2, 2, 8), ("x", "yl", "yh", "c", "z"))
    t, f, d = ("x", "yl"), ("yh", "c", "z"), ("z", "x", "yl")
    e = ("z", "yh", "c")
    return jax.shard_map(
        shards,
        mesh=cube,
        in_specs=(P(t, f), P(d, ("yh", "c")), P(t, e)),
        out_specs=(P(t, e), P(t, f), P(d, ("yh", "c"))),
        check_vma=False,
    )
```

```python
import jax
import jax.numpy as jnp
from jax import lax
from jax.experimental import pallas as pl
from jax.experimental.pallas import tpu as pltpu
from jax.sharding import Mesh
from jax.sharding import PartitionSpec as P

coeff = 0.7978845608028654
bf16 = jnp.bfloat16
f32 = jnp.float32


def gelu_value(v):
    return 0.5 * v * (1.0 + jnp.tanh(coeff * (v + 0.044715 * v * v * v)))


def gelu_slope(v):
    tval = jnp.tanh(coeff * (v + 0.044715 * v * v * v))
    return 0.5 * (1.0 + tval) + 0.5 * v * (1.0 - tval * tval) * coeff * (
        1.0 + 3.0 * 0.044715 * v * v
    )


def swap_y(a, mask):
    flip = (mask & 1) * 2 + (mask >> 1)
    return lax.ppermute(a, ("yl", "yh"), [(i, i ^ flip) for i in range(4)])


def swap_x(a, mask):
    return lax.ppermute(a, "x", [(i, i ^ mask) for i in range(4)])


def swap_c(a):
    return lax.ppermute(a, "c", [(0, 1), (1, 0)])


def gather4(swap, own):
    return [own] + [swap(own, m) for m in (1, 2, 3)]


def scatter4(swap, blocks):
    total = blocks[0].astype(f32)
    for m in (1, 3, 2):
        total = total + swap(blocks[m], m).astype(f32)
    return total.astype(bf16)


def add(a, b):
    return (a.astype(f32) + b.astype(f32)).astype(bf16)


def near4(swap, own):
    return swap(own, 1), swap(own, 3)


def far4(swap, near1, near3):
    half = near1.shape[0] // 2
    return swap(near1[:half], 3), swap(near3[half:], 1)


def scatter_far(swap, far):
    half = far.shape[0] // 2
    return swap(far[:half], 1), swap(far[half:], 3)


def scatter_near(near1, near3, far1, far3):
    half = far1.shape[0]
    near3 = jnp.concatenate([add(near3[:half], far1), near3[half:]], axis=0)
    near1 = jnp.concatenate([near1[:half], add(near1[half:], far3)], axis=0)
    return near1, near3


def add3(own, got1, got3):
    return own.astype(f32) + got1.astype(f32) + got3.astype(f32)


def after(value, *others):
    return lax.optimization_barrier((value,) + others)[0]


def split_kernel(which_ref, a_ref, mine_ref, theirs_ref):
    which = which_ref[0]
    for value, low_ref, high_ref in ((0, mine_ref, theirs_ref), (1, theirs_ref, mine_ref)):

        @pl.when(which == value)
        def _(low_ref=low_ref, high_ref=high_ref):
            for k in range(a_ref.shape[1] // 768):
                low_ref[:, 384 * k : 384 * k + 384] = a_ref[:, 768 * k : 768 * k + 384]
                high_ref[:, 384 * k : 384 * k + 384] = a_ref[:, 768 * k + 384 : 768 * k + 768]


def split_columns(a, which):
    half = jax.ShapeDtypeStruct((a.shape[0], a.shape[1] // 2), a.dtype)
    return pl.pallas_call(
        split_kernel,
        out_shape=(half, half),
        in_specs=[pl.BlockSpec(memory_space=pltpu.SMEM), pl.BlockSpec(memory_space=pltpu.VMEM)],
        out_specs=(pl.BlockSpec(memory_space=pltpu.VMEM),) * 2,
        cost_estimate=pl.CostEstimate(flops=0, bytes_accessed=4 * a.size, transcendentals=0),
    )(which.astype(jnp.int32).reshape(1), a)


def join_columns(mine, theirs, which):
    low = jnp.where(which == 0, mine, theirs)
    high = jnp.where(which == 0, theirs, mine)
    n = mine.shape[1] // 384
    return jnp.concatenate([p[:, 384 * k : 384 * k + 384] for k in range(n) for p in (low, high)], axis=1)


def shards(pre_act, down_weight, grad_out):
    x, yl, yh, c = (lax.axis_index(n) for n in ("x", "yl", "yh", "c"))
    pre32 = pre_act.astype(f32)
    hid = gelu_value(pre32).astype(bf16)
    low, high = hid[:, :384], hid[:, 384:]
    keep, give = jnp.where(yl == 0, low, high), jnp.where(yl == 0, high, low)
    got_h = swap_y(give, 1)

    keep_w, give_w = split_columns(after(down_weight, give), yl)
    got_w = swap_y(give_w, 1)
    hidden = lax.all_gather(jnp.concatenate([keep, after(got_h, keep_w)], axis=0), "z", axis=1, tiled=True)
    own = jnp.concatenate([keep_w, got_w], axis=0)
    near = near4(swap_x, after(own, got_h))
    weight = jnp.concatenate([own, near[0], *far4(swap_x, *near), near[1]], axis=0)

    got = gather4(swap_y, after(grad_out.T, near[0]))
    part = jnp.stack([jnp.concatenate([got[2 * h], got[2 * h + 1]], axis=1) for h in range(2)])
    table = jnp.concatenate([part, swap_c(part)], axis=0).reshape(8, 96, 1024)
    flip = x ^ (yh * 2 + c)
    iota = jnp.arange(8, dtype=jnp.int32)
    place = flip ^ (iota >> 1)
    grads = table[(place & 1) * 4 + (place >> 1) * 2 + (yl ^ (iota & 1))].reshape(768, 1024)

    gh = lax.dot_general(weight, grads, (((0,), (0,)), ((), ())), preferred_element_type=f32).astype(bf16)
    gh = lax.psum_scatter(after(gh, hidden), "z", scatter_dimension=0, tiled=True)
    theirs = swap_y(gh[:, 512:], 1)
    grad_hidden = join_columns(gh[:, :512].T, theirs.T, yl)
    grad_pre = (grad_hidden.astype(f32) * gelu_slope(pre32)).astype(bf16)

    gw_all = jnp.dot(grads, hidden, preferred_element_type=f32).astype(bf16)
    gw = gw_all.reshape(4, 192, 3072)
    far = scatter_far(swap_x, gw[2])
    out = lax.dot_general(weight, after(hidden, gw_all), (((1,), (1,)), ((), ())), preferred_element_type=f32)
    out = out.astype(bf16).reshape(8, 96, 1024)
    passed = scatter_near(gw[1], gw[3], after(far[0], out), after(far[1], out))
    near = swap_x(passed[0], 1), swap_x(passed[1], 3)
    order = (flip ^ (((iota >> 1) & 1) * 2 + (iota >> 2))) * 2 + ((iota & 1) ^ yl)
    part = add(out[order[:4]], swap_c(out[order[4:]])).reshape(2, 192, 1024)
    output = scatter4(swap_y, [part[m >> 1, :, (m & 1) * 512 : (m & 1) * 512 + 512] for m in range(4)])
    total = add3(after(gw[0], output), *near).astype(bf16)
    grad_weight = join_columns(after(total[:96], theirs), swap_y(total[96:], 1), yl)
    output = output.T
    return output, grad_pre, grad_weight


def solution(mesh):
    cube = Mesh(mesh.devices.reshape(4, 2, 2, 2, 8), ("x", "yl", "yh", "c", "z"))
    t, f, d = ("x", "yl"), ("yh", "c", "z"), ("z", "x", "yl")
    e = ("z", "yh", "c")
    return jax.shard_map(
        shards,
        mesh=cube,
        in_specs=(P(t, f), P(d, ("yh", "c")), P(t, e)),
        out_specs=(P(t, e), P(t, f), P(d, ("yh", "c"))),
        check_vma=False,
    )
```

```python
import jax
import jax.numpy as jnp
from jax import lax
from jax.experimental import pallas as pl
from jax.experimental.pallas import tpu as pltpu
from jax.sharding import Mesh
from jax.sharding import PartitionSpec as P

coeff = 0.7978845608028654
bf16 = jnp.bfloat16
f32 = jnp.float32


def gelu_value(v):
    return 0.5 * v * (1.0 + jnp.tanh(coeff * (v + 0.044715 * v * v * v)))


def gelu_slope(v):
    tval = jnp.tanh(coeff * (v + 0.044715 * v * v * v))
    return 0.5 * (1.0 + tval) + 0.5 * v * (1.0 - tval * tval) * coeff * (
        1.0 + 3.0 * 0.044715 * v * v
    )


def swap_y(a, mask):
    flip = (mask & 1) * 2 + (mask >> 1)
    return lax.ppermute(a, ("yl", "yh"), [(i, i ^ flip) for i in range(4)])


def swap_x(a, mask):
    return lax.ppermute(a, "x", [(i, i ^ mask) for i in range(4)])


def swap_c(a):
    return lax.ppermute(a, "c", [(0, 1), (1, 0)])


def gather4(swap, own):
    return [own] + [swap(own, m) for m in (1, 2, 3)]


def scatter4(swap, blocks):
    total = blocks[0].astype(f32)
    for m in (1, 3, 2):
        total = total + swap(blocks[m], m).astype(f32)
    return total.astype(bf16)


def add(a, b):
    return (a.astype(f32) + b.astype(f32)).astype(bf16)


def near4(swap, own):
    return swap(own, 1), swap(own, 3)


def far4(swap, near1, near3):
    half = near1.shape[0] // 2
    return swap(near1[:half], 3), swap(near3[half:], 1)


def scatter_far(swap, far):
    half = far.shape[0] // 2
    return swap(far[:half], 1), swap(far[half:], 3)


def scatter_near(near1, near3, far1, far3):
    half = far1.shape[0]
    near3 = jnp.concatenate([add(near3[:half], far1), near3[half:]], axis=0)
    near1 = jnp.concatenate([near1[:half], add(near1[half:], far3)], axis=0)
    return near1, near3


def add3(own, got1, got3):
    return own.astype(f32) + got1.astype(f32) + got3.astype(f32)


def after(value, *others):
    return lax.optimization_barrier((value,) + others)[0]


def split_kernel(which_ref, a_ref, mine_ref, theirs_ref):
    which = which_ref[0]
    for value, low_ref, high_ref in ((0, mine_ref, theirs_ref), (1, theirs_ref, mine_ref)):

        @pl.when(which == value)
        def _(low_ref=low_ref, high_ref=high_ref):
            for k in range(a_ref.shape[1] // 768):
                low_ref[:, 384 * k : 384 * k + 384] = a_ref[:, 768 * k : 768 * k + 384]
                high_ref[:, 384 * k : 384 * k + 384] = a_ref[:, 768 * k + 384 : 768 * k + 768]


def split_columns(a, which):
    half = jax.ShapeDtypeStruct((a.shape[0], a.shape[1] // 2), a.dtype)
    return pl.pallas_call(
        split_kernel,
        out_shape=(half, half),
        in_specs=[pl.BlockSpec(memory_space=pltpu.SMEM), pl.BlockSpec(memory_space=pltpu.VMEM)],
        out_specs=(pl.BlockSpec(memory_space=pltpu.VMEM),) * 2,
        cost_estimate=pl.CostEstimate(flops=0, bytes_accessed=4 * a.size, transcendentals=0),
    )(which.astype(jnp.int32).reshape(1), a)


def join_columns(mine, theirs, which):
    low = jnp.where(which == 0, mine, theirs)
    high = jnp.where(which == 0, theirs, mine)
    n = mine.shape[1] // 384
    return jnp.concatenate([p[:, 384 * k : 384 * k + 384] for k in range(n) for p in (low, high)], axis=1)


def shards(pre_act, down_weight, grad_out):
    x, yl, yh, c = (lax.axis_index(n) for n in ("x", "yl", "yh", "c"))
    pre32 = pre_act.astype(f32)
    low, high = pre_act[:, :384], pre_act[:, 384:]
    keep, give = jnp.where(yl == 0, low, high), jnp.where(yl == 0, high, low)
    got_h = swap_y(give, 1)

    keep_w, give_w = split_columns(after(down_weight, give), yl)
    got_w = swap_y(give_w, 1)
    hid = jnp.concatenate([keep, after(got_h, keep_w)], axis=0)
    hid = gelu_value(hid.astype(f32)).astype(bf16)
    hidden = lax.all_gather(hid, "z", axis=1, tiled=True)
    own = jnp.concatenate([keep_w, got_w], axis=0)
    near = near4(swap_x, after(own, got_h))
    weight = jnp.concatenate([own, near[0], *far4(swap_x, *near), near[1]], axis=0)

    got = gather4(swap_y, after(grad_out.T, near[0]))
    part = jnp.stack([jnp.concatenate([got[2 * h], got[2 * h + 1]], axis=1) for h in range(2)])
    table = jnp.concatenate([part, swap_c(part)], axis=0).reshape(8, 96, 1024)
    flip = x ^ (yh * 2 + c)
    iota = jnp.arange(8, dtype=jnp.int32)
    place = flip ^ (iota >> 1)
    grads = table[(place & 1) * 4 + (place >> 1) * 2 + (yl ^ (iota & 1))].reshape(768, 1024)

    gh = lax.dot_general(weight, grads, (((0,), (0,)), ((), ())), preferred_element_type=f32).astype(bf16)
    gh = lax.psum_scatter(gh, "z", scatter_dimension=0, tiled=True)
    gw_all = jnp.dot(grads, hidden, preferred_element_type=f32).astype(bf16)
    gw = gw_all.reshape(4, 192, 3072)
    far = scatter_far(swap_x, gw[2])
    out = lax.dot_general(weight, after(hidden, gw_all), (((1,), (1,)), ((), ())), preferred_element_type=f32)
    out = out.astype(bf16).reshape(8, 96, 1024)
    passed = scatter_near(gw[1], gw[3], after(far[0], out), after(far[1], out))
    near = swap_x(passed[0], 1), swap_x(passed[1], 3)
    order = (flip ^ (((iota >> 1) & 1) * 2 + (iota >> 2))) * 2 + ((iota & 1) ^ yl)
    part = add(out[order[:4]], swap_c(out[order[4:]])).reshape(2, 192, 1024)
    output = scatter4(swap_y, [part[m >> 1, :, (m & 1) * 512 : (m & 1) * 512 + 512] for m in range(4)])
    total = add3(after(gw[0], output), *near).astype(bf16)
    got_gw = swap_y(total[96:], 1)
    theirs = swap_y(after(gh, got_gw)[:, 512:], 1)
    grad_hidden = join_columns(gh[:, :512].T, theirs.T, yl)
    grad_pre = (grad_hidden.astype(f32) * gelu_slope(pre32)).astype(bf16)
    grad_weight = join_columns(total[:96], got_gw, yl)
    output = output.T
    return output, grad_pre, grad_weight


def solution(mesh):
    cube = Mesh(mesh.devices.reshape(4, 2, 2, 2, 8), ("x", "yl", "yh", "c", "z"))
    t, f, d = ("x", "yl"), ("yh", "c", "z"), ("z", "x", "yl")
    e = ("z", "yh", "c")
    return jax.shard_map(
        shards,
        mesh=cube,
        in_specs=(P(t, f), P(d, ("yh", "c")), P(t, e)),
        out_specs=(P(t, e), P(t, f), P(d, ("yh", "c"))),
        check_vma=False,
    )
```

```python
import jax
import jax.numpy as jnp
from jax import lax
from jax.experimental import pallas as pl
from jax.experimental.pallas import tpu as pltpu
from jax.sharding import Mesh
from jax.sharding import PartitionSpec as P

coeff = 0.7978845608028654
bf16 = jnp.bfloat16
f32 = jnp.float32


def gelu_value(v):
    return 0.5 * v * (1.0 + jnp.tanh(coeff * (v + 0.044715 * v * v * v)))


def gelu_slope(v):
    tval = jnp.tanh(coeff * (v + 0.044715 * v * v * v))
    return 0.5 * (1.0 + tval) + 0.5 * v * (1.0 - tval * tval) * coeff * (
        1.0 + 3.0 * 0.044715 * v * v
    )


def swap_y(a, mask):
    flip = (mask & 1) * 2 + (mask >> 1)
    return lax.ppermute(a, ("yl", "yh"), [(i, i ^ flip) for i in range(4)])


def swap_x(a, mask):
    return lax.ppermute(a, "x", [(i, i ^ mask) for i in range(4)])


def swap_c(a):
    return lax.ppermute(a, "c", [(0, 1), (1, 0)])


def gather4(swap, own):
    return [own] + [swap(own, m) for m in (1, 2, 3)]


def scatter4(swap, blocks):
    total = blocks[0].astype(f32)
    for m in (1, 3, 2):
        total = total + swap(blocks[m], m).astype(f32)
    return total.astype(bf16)


def add(a, b):
    return (a.astype(f32) + b.astype(f32)).astype(bf16)


def near4(swap, own):
    return swap(own, 1), swap(own, 3)


def far4(swap, near1, near3):
    half = near1.shape[0] // 2
    return swap(near1[:half], 3), swap(near3[half:], 1)


def scatter_far(swap, far):
    half = far.shape[0] // 2
    return swap(far[:half], 1), swap(far[half:], 3)


def scatter_near(near1, near3, far1, far3):
    half = far1.shape[0]
    near3 = jnp.concatenate([add(near3[:half], far1), near3[half:]], axis=0)
    near1 = jnp.concatenate([near1[:half], add(near1[half:], far3)], axis=0)
    return near1, near3


def add3(own, got1, got3):
    return own.astype(f32) + got1.astype(f32) + got3.astype(f32)


def after(value, *others):
    return lax.optimization_barrier((value,) + others)[0]


def split_kernel(which_ref, a_ref, mine_ref, theirs_ref):
    which = which_ref[0]
    for value, low_ref, high_ref in ((0, mine_ref, theirs_ref), (1, theirs_ref, mine_ref)):

        @pl.when(which == value)
        def _(low_ref=low_ref, high_ref=high_ref):
            for k in range(a_ref.shape[1] // 768):
                low_ref[:, 384 * k : 384 * k + 384] = a_ref[:, 768 * k : 768 * k + 384]
                high_ref[:, 384 * k : 384 * k + 384] = a_ref[:, 768 * k + 384 : 768 * k + 768]


def split_columns(a, which):
    half = jax.ShapeDtypeStruct((a.shape[0], a.shape[1] // 2), a.dtype)
    return pl.pallas_call(
        split_kernel,
        out_shape=(half, half),
        in_specs=[pl.BlockSpec(memory_space=pltpu.SMEM), pl.BlockSpec(memory_space=pltpu.VMEM)],
        out_specs=(pl.BlockSpec(memory_space=pltpu.VMEM),) * 2,
        cost_estimate=pl.CostEstimate(flops=0, bytes_accessed=4 * a.size, transcendentals=0),
    )(which.astype(jnp.int32).reshape(1), a)


def join_columns(mine, theirs, which):
    low = jnp.where(which == 0, mine, theirs)
    high = jnp.where(which == 0, theirs, mine)
    n = mine.shape[1] // 384
    return jnp.concatenate([p[:, 384 * k : 384 * k + 384] for k in range(n) for p in (low, high)], axis=1)


def shards(pre_act, down_weight, grad_out):
    x, yl, yh, c = (lax.axis_index(n) for n in ("x", "yl", "yh", "c"))
    pre32 = pre_act.astype(f32)
    low, high = pre_act[:, :384], pre_act[:, 384:]
    keep, give = jnp.where(yl == 0, low, high), jnp.where(yl == 0, high, low)
    got_h = swap_y(give, 1)

    keep_w, give_w = split_columns(after(down_weight, give), yl)
    got_w = swap_y(give_w, 1)
    hid = jnp.concatenate([keep, after(got_h, keep_w)], axis=0)
    hid = gelu_value(hid.astype(f32)).astype(bf16)
    hidden = lax.all_gather(hid, "z", axis=1, tiled=True)
    own = jnp.concatenate([keep_w, got_w], axis=0)
    near = near4(swap_x, after(own, got_h))
    weight = jnp.concatenate([own, near[0], *far4(swap_x, *near), near[1]], axis=0)

    got = gather4(swap_y, after(grad_out.T, near[0]))
    part = jnp.stack([jnp.concatenate([got[2 * h], got[2 * h + 1]], axis=1) for h in range(2)])
    table = jnp.concatenate([part, swap_c(part)], axis=0).reshape(8, 96, 1024)
    flip = x ^ (yh * 2 + c)
    iota = jnp.arange(8, dtype=jnp.int32)
    place = flip ^ (iota >> 1)
    grads = table[(place & 1) * 4 + (place >> 1) * 2 + (yl ^ (iota & 1))].reshape(768, 1024)

    gh = lax.dot_general(weight, grads, (((0,), (0,)), ((), ())), preferred_element_type=f32).astype(bf16)
    gh = lax.psum_scatter(gh, "z", scatter_dimension=0, tiled=True)
    gw_all = jnp.dot(grads, hidden, preferred_element_type=f32).astype(bf16)
    gw = gw_all.reshape(4, 192, 3072)
    far = scatter_far(swap_x, gw[2])
    out = lax.dot_general(weight, after(hidden, gw_all), (((1,), (1,)), ((), ())), preferred_element_type=f32)
    out = out.astype(bf16).reshape(8, 96, 1024)
    passed = scatter_near(gw[1], gw[3], after(far[0], out), after(far[1], out))
    near = swap_x(passed[0], 1), swap_x(passed[1], 3)
    order = (flip ^ (((iota >> 1) & 1) * 2 + (iota >> 2))) * 2 + ((iota & 1) ^ yl)
    part = add(out[order[:4]], swap_c(out[order[4:]])).reshape(2, 192, 1024)
    output = scatter4(swap_y, [part[m >> 1, :, (m & 1) * 512 : (m & 1) * 512 + 512] for m in range(4)])
    total = add3(after(gw[0], output), *near).astype(bf16)
    got_gw = swap_y(total[96:], 1)
    theirs = swap_y(after(gh[:, 512:], got_gw), 1)
    grad_hidden = join_columns(gh[:, :512].T, theirs.T, yl)
    grad_pre = (grad_hidden.astype(f32) * gelu_slope(pre32)).astype(bf16)
    grad_weight = join_columns(total[:96], got_gw, yl)
    output = output.T
    return output, grad_pre, grad_weight


def solution(mesh):
    cube = Mesh(mesh.devices.reshape(4, 2, 2, 2, 8), ("x", "yl", "yh", "c", "z"))
    t, f, d = ("x", "yl"), ("yh", "c", "z"), ("z", "x", "yl")
    e = ("z", "yh", "c")
    return jax.shard_map(
        shards,
        mesh=cube,
        in_specs=(P(t, f), P(d, ("yh", "c")), P(t, e)),
        out_specs=(P(t, e), P(t, f), P(d, ("yh", "c"))),
        check_vma=False,
    )
```
